256 devices in a mesh: sweep: 16 (over y, x), cross: 2 (over core), band: 8 (over z).
Axes of the slice: x: 4, y: 4, z: 8, core: 2. Of those that a mesh axis runs over, the one named last changes fastest.
Arguments:
- operator: float32 [8, 16, 1024, 512], P('band', 'sweep', 'cross'), may hold values from -0.375 to 0.375
- source: float32 [8, 16, 1024, 512], P('band', 'sweep', 'cross'), may hold values from -6 to 6
- sky: float32 [8, 1024, 512], P('band', 'cross'), may hold values from -6 to 6
- response: float32 [8, 16, 1024, 512], P('band', 'sweep', 'cross'), may hold values from -6 to 6
- extinction: float32 [8], P('band'), may hold values from 0.2 to 1
- leaf_density: float32 [16], replicated, may hold values from 0.1 to 1.5
- leaf_class: int32 [16, 1024], P('sweep', 'cross'), may hold values from 0 to 15
- occupied: int32 [16, 1024], P('sweep', 'cross'), may hold values 0 or 1
Outputs:
- observed: float32 [8, 16, 1024, 512], P('band', 'sweep', 'cross')
- lai_grad: float32 [16, 1024], P('sweep', 'cross')
The draws below stay inside these ranges and needn't reach their ends.
All inputs are finite; a program needn't handle non-finite values. No bound on the sum of `occupied` on one device may be relied on, other than what follows from the above.
Results may differ from the reference program's by a relative error of at most 0.00023.
Values sent between devices are 32-bit elements; how exact they have to be, the bound alone decides.
No kernel may reach another device: no remote copies, remote signals or barrier semaphores. Data moves between devices by JAX's collectives and lax.ppermute only.
A program may use at most 192 MiB of HBM per device.

```python
import math
import jax
import jax.numpy as jnp
from jax import lax

FC = 16
FV = 32
K = 512
R = 512
CLASSES = 16
BANDS = 8
TILES_S = 16
TILES_C = 2


def with_ends(values, rng, low, top_value):
    longest = values.shape.index(max(values.shape))
    spots = []
    for shift in (0, 1):
        where = [jax.random.randint(jax.random.fold_in(rng, axis), (), 0, length) for axis, length in enumerate(values.shape)]
        where[longest] = (where[longest] + shift) % values.shape[longest]
        spots.append(tuple(where))
    return values.at[spots[0]].set(low).at[spots[1]].set(top_value)


def levels(own_key, dims, shards, low, largest):
    gain = 1.0
    for axis_at, parts in shards:
        heights = jax.random.uniform(jax.random.fold_in(jax.random.fold_in(own_key, 6), axis_at), (parts,), jnp.float32, low / len(shards), largest / len(shards))
        gain = gain * jnp.repeat(jnp.exp(heights), dims[axis_at] // parts).reshape((-1,) + (1,) * (len(dims) - 1 - axis_at))
    return gain


def noise(own_key, extent, width, bound, cuts=(), held_as=jnp.bfloat16):
    factor_of = levels(own_key, extent, cuts, -0.22, 0.18) if cuts else 1.0
    result = jax.random.normal(own_key, extent, jnp.float32) * width * factor_of
    return jnp.minimum(jnp.maximum(result, -bound), bound).astype(held_as)


def setup_inputs(seed: int = 0) -> dict:
    streams_of = jax.random.split(jax.random.key(seed), 9)
    return {
        "operator": noise(streams_of[0], (BANDS, TILES_S, TILES_C * K, K), (K // 2) ** -0.5, 0.375, ((0, 8), (1, 16), (2, 2)), jnp.float32),
        "source": noise(streams_of[1], (BANDS, TILES_S, TILES_C * K, R), 1.0, 6.0, ((0, 8), (1, 16), (2, 2)), jnp.float32),
        "sky": noise(streams_of[2], (BANDS, TILES_C * K, R), 1.0, 6.0, ((0, 8), (1, 2)), jnp.float32),
        "response": noise(streams_of[3], (BANDS, TILES_S, TILES_C * K, R), 1.0, 6.0, ((0, 8), (1, 16), (2, 2)), jnp.float32),
        "extinction": jnp.clip(jnp.exp(math.log(1.0) - 1.609438 * jax.random.uniform(streams_of[4], (BANDS,), jnp.float32) ** levels(streams_of[4], (BANDS,), ((0, 8),), -0.2, 0.2)), 0.2, 1.0),
        "leaf_density": jnp.clip(jnp.exp(jax.random.uniform(streams_of[5], (CLASSES,), jnp.float32, math.log(0.1), math.log(1.5))), 0.1, 1.5),
        "leaf_class": with_ends(jax.random.randint(streams_of[6], (TILES_S, TILES_C * K), 0, CLASSES), jax.random.fold_in(streams_of[6], 1), 0, CLASSES - 1).astype(jnp.int32),
        "occupied": with_ends((jax.random.randint(streams_of[7], (TILES_S, TILES_C * K), 0, 8) < 1).astype(jnp.int32), jax.random.fold_in(streams_of[7], 1), 0, 1),
    }


lateral_weight = 0.25

def lateral(field):
    grid = field.reshape(BANDS, TILES_S, TILES_C * FC, FV * R)
    padded = jnp.pad(grid, ((0, 0), (0, 0), (1, 1), (0, 0)))
    smooth = grid + lateral_weight * (padded[:, :, :-2] + padded[:, :, 2:] - 2.0 * grid)
    return smooth.reshape(field.shape)

def reference(operator, source, sky, response, extinction, leaf_density, leaf_class, occupied):
    density = leaf_density[leaf_class]
    open_cells = (1 - occupied).astype(jnp.float32)
    transmit = open_cells[None] * jnp.exp(-extinction[:, None, None] * density[None])
    tiles = operator.reshape(BANDS, TILES_S, TILES_C, K, K)
    attenuated = transmit.reshape(BANDS, TILES_S, TILES_C, K, 1) * tiles
    emitted = source.reshape(BANDS, TILES_S, TILES_C, K, R)
    highest = lax.Precision.HIGHEST
    state = sky.reshape(BANDS, TILES_C, K, R)
    inputs = []
    outputs = []
    for sweep_tile in range(TILES_S):
        inputs.append(state)
        state = jnp.einsum('bckj,bcjr->bckr', attenuated[:, sweep_tile], state, precision=highest) + emitted[:, sweep_tile]
        outputs.append(state)
    radiance = jnp.stack(outputs, axis=1).reshape(source.shape)
    observed = lateral(radiance)
    cotangent = (lateral(response) / math.sqrt(R)).reshape(BANDS, TILES_S, TILES_C, K, R)
    carried = jnp.zeros((BANDS, TILES_C, K, R), jnp.float32)
    grads = [None] * TILES_S
    trans_tiles = transmit.reshape(BANDS, TILES_S, TILES_C, K)
    for sweep_tile in reversed(range(TILES_S)):
        adjoint = cotangent[:, sweep_tile] + carried
        carried = jnp.einsum('bcjk,bcjr->bckr', attenuated[:, sweep_tile], adjoint, precision=highest)
        pushed = jnp.einsum('bckj,bcjr->bckr', tiles[:, sweep_tile], inputs[sweep_tile], precision=highest)
        along = lax.optimization_barrier(jnp.sum(adjoint * pushed, axis=-1))
        term = -extinction[:, None, None] * trans_tiles[:, sweep_tile] * along
        grads[sweep_tile] = lax.optimization_barrier(jnp.sum(term, axis=0)).reshape(TILES_C * K)
    lai_grad = jnp.stack(grads, axis=0)
    return (observed, lai_grad)
```

```python
import functools
import math

import jax
import jax.numpy as jnp
from jax import lax
from jax.experimental import pallas as pl
from jax.experimental.pallas import tpu as pltpu
from jax.sharding import PartitionSpec as P

K = 512
R = 512
FV = 32
ROW = 4
ROWS = 4
CH = R // ROW
BANDS = 8
CROSS = 2
F32 = jnp.float32
BF16 = jnp.bfloat16
NT = (((1,), (1,)), ((), ()))
NN = (((1,), (0,)), ((), ()))
PARAMS = pltpu.CompilerParams(vmem_limit_bytes=56 * 1024 * 1024)

X_RING = {
    d: [(ROW * y + x, ROW * y + (x + d) % ROW) for y in range(ROWS) for x in range(ROW)] for d in range(1, ROW)
}
SWAP = [1, 0, 3, 2]
TURN = [3, 2, 1, 0]
Y_SWAP = [(ROW * y + x, ROW * SWAP[y] + x) for y in range(ROWS) for x in range(ROW)]
Y_TURN = [(ROW * y + x, ROW * TURN[y] + x) for y in range(ROWS) for x in range(ROW)]


def shift_x(value, by):
    return lax.ppermute(value, "sweep", X_RING[by % ROW])


def call(body, outs, *args, scratch=()):
    scalar = pl.BlockSpec(memory_space=pltpu.SMEM)
    vector = pl.BlockSpec(memory_space=pltpu.VMEM)
    return pl.pallas_call(
        body,
        out_shape=[jax.ShapeDtypeStruct(shape, dtype) for shape, dtype in outs],
        in_specs=[scalar if arg.ndim == 1 else vector for arg in args],
        out_specs=[vector] * len(outs),
        scratch_shapes=list(scratch),
        compiler_params=PARAMS,
    )(*args)


def place():
    at = lax.axis_index("sweep")
    return at % ROW, at // ROW


def split(value):
    high = value.astype(BF16)
    return high, (value - high.astype(F32)).astype(BF16)


def times(rows, high, low, dims):
    rows_high, rows_low = split(rows)
    count = rows.shape[0]
    both = lax.dot_general(
        jnp.concatenate([rows_high, rows_low], axis=0), high, dims, preferred_element_type=F32
    )
    cross = lax.dot_general(rows_high, low, dims, preferred_element_type=F32)
    return both[:count] + (both[count:] + cross)


def spread_body(source, response, before, after, sky, first, second, sky_rays):
    x, y = place()
    upsun = y < 2
    scale = 1.0 / math.sqrt(R)
    weights = response[...]
    up = jnp.concatenate([before[...], weights[:-FV]], axis=0)
    down = jnp.concatenate([weights[FV:], after[...]], axis=0)
    cot = (0.5 * weights + 0.25 * (up + down)) * scale
    for chunk in range(ROW):
        dist = (chunk - x + ROW) % ROW
        cols = slice(chunk * CH, (chunk + 1) * CH)
        emitted = source[:, cols].T
        cotangent = cot[:, cols].T
        first[dist] = jnp.where(upsun, emitted, cotangent)
        second[dist] = jnp.where(upsun, cotangent, emitted)
    sky_rays[...] = sky[:, pl.ds(pl.multiple_of(x * CH, CH), CH)].T


def forward_chain(high, low, emitted, incoming, keep):
    def step(j, state):
        gained = times(state, high[j], low[j], NT)
        state = gained + emitted[j]
        keep(j, gained, state)
        return state

    return lax.fori_loop(0, ROW, step, incoming)


def backward_chain(high, low, cotangent, incoming, keep, through):
    def step(i, state):
        j = ROW - 1 - i
        adjoint = cotangent[j] + state
        keep(j, adjoint)
        return times(adjoint, high[j], low[j], NN)

    state = lax.fori_loop(0, ROW - 1, step, incoming)
    adjoint = cotangent[0] + state
    keep(0, adjoint)
    if through:
        return times(adjoint, high[0], low[0], NN)
    return None


def start_body(own, left_top, left_bottom, right_top, right_bottom, far_top, far_bottom, e0, e1, e2, e3, sky_rays,
               high, low, given, saved, radiance, out):
    x, y = place()
    half = K // 2
    for dist, parts in enumerate(((own,), (left_top, left_bottom), (far_top, far_bottom), (right_top, right_bottom))):
        tile = (x - dist + ROW) % ROW
        size = K // len(parts)
        for at, part in enumerate(parts):
            part_high, part_low = split(part[...])
            high[tile, at * size:(at + 1) * size] = part_high
            low[tile, at * size:(at + 1) * size] = part_low
    for dist, part in enumerate((e0, e1, e2, e3)):
        given[(x - dist + ROW) % ROW] = part[...]

    @pl.when(y == 0)
    def _():
        def keep(j, gained, state):
            saved[j] = gained
            radiance[j] = state

        out[...] = forward_chain(high, low, given, sky_rays[...], keep)

    @pl.when(y == ROWS - 1)
    def _():
        def keep(j, adjoint):
            saved[j] = adjoint

        out[...] = backward_chain(high, low, given, jnp.zeros((CH, K), F32), keep, True)


def ends(high, low, given, y, forward_row, out):
    @pl.when(y == forward_row)
    def _():
        def step(j, state):
            return times(state, high[j], low[j], NT) + given[j]

        out[...] = lax.fori_loop(1, ROW, step, given[0])

    @pl.when(y == ROWS - 1 - forward_row)
    def _():
        out[...] = backward_chain(high, low, given, jnp.zeros((CH, K), F32), lambda j, a: None, True)


def compose_body(high, low, given, whole_high, whole_low, added):
    _, y = place()

    @pl.when((y == 1) | (y == 2))
    def _():
        def pair(at):
            return times(high[at + 1].astype(F32) + low[at + 1].astype(F32), high[at], low[at], NN)

        first_high, first_low = split(pair(0))
        whole = times(pair(2), first_high, first_low, NN)
        whole_high[...], whole_low[...] = split(whole)

    ends(high, low, given, y, 1, added)


def later_body(high, low, s0, s1, s2, s3, given, added):
    x, y = place()
    for dist, part in enumerate((s0, s1, s2, s3)):
        given[(x - dist + ROW) % ROW] = part[...]
    ends(high, low, given, y, 2, added)


def pass_body(forward_row, incoming, whole_high, whole_low, added, out):
    _, y = place()

    @pl.when(y == forward_row)
    def _():
        out[...] = times(incoming[...], whole_high[...], whole_low[...], NT) + added[...]

    @pl.when(y == ROWS - 1 - forward_row)
    def _():
        out[...] = times(incoming[...], whole_high[...], whole_low[...], NN) + added[...]


def middle_body(high, low, given, later, first_in, second_in, radiance, along, saved):
    _, y = place()
    for row, emitted, cotangent, state, adjoint_in in (
        (1, given, later, first_in, second_in),
        (2, later, given, second_in, first_in),
    ):
        @pl.when(y == row)
        def _():
            def keep_state(j, gained, new_state):
                saved[j] = gained
                radiance[j] = new_state

            def keep_adjoint(j, adjoint):
                along[j] = jnp.sum(adjoint * saved[j], axis=0, keepdims=True)

            forward_chain(high, low, emitted, state[...], keep_state)
            backward_chain(high, low, cotangent, adjoint_in[...], keep_adjoint, False)


def last_body(coeff, high, low, later, last_in, saved, early, middle, middle_along, out, along):
    x, y = place()
    factor = -coeff[0]

    @pl.when(y == 0)
    def _():
        def keep(j, adjoint):
            along[j] = factor * jnp.sum(adjoint * saved[j], axis=0, keepdims=True)

        backward_chain(high, low, later, last_in[...], keep, False)

    @pl.when(y == ROWS - 1)
    def _():
        def keep(j, gained, state):
            along[j] = factor * jnp.sum(gained * saved[j], axis=0, keepdims=True)
            out[(j - x + ROW) % ROW] = state

        forward_chain(high, low, later, last_in[...], keep)

    @pl.when(y == 0)
    def _():
        for j in range(ROW):
            out[(j - x + ROW) % ROW] = early[j]

    @pl.when((y == 1) | (y == 2))
    def _():
        for j in range(ROW):
            out[(j - x + ROW) % ROW] = middle[j]
            along[j] = factor * middle_along[j]


def sum_body(*refs):
    parts, out, held = refs[:BANDS], refs[BANDS], refs[BANDS + 1]
    x, _ = place()
    z = lax.axis_index("band")
    for dist, part in enumerate(parts):
        held[(z - dist + BANDS) % BANDS] = part[...]
    total = held[0]
    for band in range(1, BANDS):
        total = total + held[band]
    held[0] = total
    for dist in range(ROW):
        out[dist] = held[0, (x + dist) % ROW]


def turn_body(r0, r1, r2, r3, out, edge, grid):
    x, _ = place()
    for dist, part in enumerate((r0, r1, r2, r3)):
        chunk = (x - dist + ROW) % ROW
        grid[:, pl.ds(pl.multiple_of(chunk * CH, CH), CH)] = part[...].T
    whole = grid[...]
    zero = jnp.zeros((FV, R), F32)
    up = jnp.concatenate([zero, whole[:-FV]], axis=0)
    down = jnp.concatenate([whole[FV:], zero], axis=0)
    out[...] = 0.5 * whole + 0.25 * (up + down)
    edge[...] = jnp.where(lax.axis_index("cross") == 0, whole[-FV:], whole[:FV])


def per_device(operator, source, sky, response, extinction, leaf_density, leaf_class, occupied):
    matrix = operator[0, 0]
    weights = response[0, 0]
    coeff = extinction[0]
    table_size = leaf_density.shape[0]
    density = jnp.sum(
        jnp.where(leaf_class[0][:, None] == jnp.arange(table_size)[None, :], leaf_density[None, :], 0.0), axis=1
    )
    transmit = (1 - occupied[0]).astype(F32) * jnp.exp(-coeff * density)
    local = transmit[:, None] * matrix
    side = lax.axis_index("cross")
    other_side = [(0, 1), (1, 0)]

    half = K // 2
    top, bottom = local[:half], local[half:]
    left_top = shift_x(top, 1)
    right_bottom = shift_x(bottom, -1)
    left_bottom = shift_x(bottom, 1)
    right_top = shift_x(top, -1)

    edge = lax.ppermute(jnp.where(side == 0, weights[-FV:], weights[:FV]), "cross", other_side)
    before = jnp.where(side == 1, edge, 0.0)
    after = jnp.where(side == 0, edge, 0.0)
    chunk = ((ROW, CH, K), F32)
    part = ((CH, K), F32)
    first, second, sky_rays = call(spread_body, [chunk, chunk, part], source[0, 0], weights, before, after, sky[0])
    e0 = first[0]
    e1, e2, e3 = (shift_x(first[d], d) for d in (1, 2, 3))
    far_top = shift_x(left_top, 1)
    far_bottom = shift_x(right_bottom, -1)

    operators = ((ROW, K, K), BF16)
    high, low, given, saved, early, out = call(
        start_body, [operators, operators, chunk, chunk, chunk, part],
        local, left_top, left_bottom, right_top, right_bottom, far_top, far_bottom, e0, e1, e2, e3, sky_rays)
    first_in = lax.ppermute(out, "sweep", Y_SWAP)
    s0 = second[0]
    s1, s2, s3 = (shift_x(second[d], d) for d in (1, 2, 3))
    whole = ((K, K), BF16)
    whole_high, whole_low, added = call(compose_body, [whole, whole, part], high, low, given)
    (out,) = call(functools.partial(pass_body, 1), [part], first_in, whole_high, whole_low, added)
    second_in = lax.ppermute(out, "sweep", Y_TURN)
    later, added = call(later_body, [chunk, part], high, low, s0, s1, s2, s3)
    (out,) = call(functools.partial(pass_body, 2), [part], second_in, whole_high, whole_low, added)
    last_in = lax.ppermute(out, "sweep", Y_SWAP)
    line = ((ROW, 1, K), F32)
    middle, middle_along = call(
        middle_body, [chunk, line], high, low, given, later, first_in, second_in,
        scratch=[pltpu.VMEM((ROW, CH, K), F32)])
    rays, along = call(last_body, [chunk, line], extinction, high, low, later, last_in, saved, early, middle, middle_along)

    r0 = rays[0]
    r1, r2, r3 = (shift_x(rays[d], d) for d in (1, 2, 3))
    bands = [along] + [
        lax.ppermute(along, "band", [(i, (i + d) % BANDS) for i in range(BANDS)]) for d in range(1, BANDS)
    ]
    (lines,) = call(sum_body, [line], *bands, scratch=[pltpu.VMEM((BANDS, ROW, 1, K), F32)])
    total = lines[0] + shift_x(lines[1], 1) + shift_x(lines[2], 2) + shift_x(lines[3], 3)

    grid = ((K, R), F32)
    smooth, edge = call(turn_body, [grid, ((FV, R), F32)], r0, r1, r2, r3, scratch=[pltpu.VMEM((K, R), F32)])
    edge = lax.ppermute(edge, "cross", other_side)
    row = jnp.where(side == 0, K - FV, 0)
    rim = lax.dynamic_slice(smooth, (row, 0), (FV, R)) + 0.25 * edge
    observed = lax.dynamic_update_slice(smooth, rim, (row, 0))
    return (observed[None, None], total)


def solution(mesh):
    in_specs = (
        P("band", "sweep", "cross", None),
        P("band", "sweep", "cross", None),
        P("band", "cross", None),
        P("band", "sweep", "cross", None),
        P("band"),
        P(),
        P("sweep", "cross"),
        P("sweep", "cross"),
    )
    out_specs = (P("band", "sweep", "cross", None), P("sweep", "cross"))
    return jax.shard_map(
        per_device, mesh=mesh, in_specs=in_specs, out_specs=out_specs, check_vma=False
    )
```

```python
import functools
import math

import jax
import jax.numpy as jnp
from jax import lax
from jax.experimental import pallas as pl
from jax.experimental.pallas import tpu as pltpu
from jax.sharding import PartitionSpec as P

K = 512
R = 512
FV = 32
ROW = 4
ROWS = 4
CH = R // ROW
BANDS = 8
SPARE = 8
F32 = jnp.float32
BF16 = jnp.bfloat16
NT = (((1,), (1,)), ((), ()))
NN = (((1,), (0,)), ((), ()))
PARAMS = pltpu.CompilerParams(vmem_limit_bytes=24 * 1024 * 1024)

X_RING = {
    d: [(ROW * y + x, ROW * y + (x + d) % ROW) for y in range(ROWS) for x in range(ROW)] for d in range(1, ROW)
}
SWAP = [1, 0, 3, 2]
TURN = [3, 2, 1, 0]
Y_SWAP = [(ROW * y + x, ROW * SWAP[y] + x) for y in range(ROWS) for x in range(ROW)]
Y_TURN = [(ROW * y + x, ROW * TURN[y] + x) for y in range(ROWS) for x in range(ROW)]
ROW_BANDS = [[(ROW * y + x) * BANDS + z for x in range(ROW) for z in range(BANDS)] for y in range(ROWS)]


def shift_x(value, by):
    return lax.ppermute(value, "sweep", X_RING[by % ROW])


def call(body, outs, *args, scratch=()):
    scalar = pl.BlockSpec(memory_space=pltpu.SMEM)
    vector = pl.BlockSpec(memory_space=pltpu.VMEM)
    return pl.pallas_call(
        body,
        out_shape=[jax.ShapeDtypeStruct(shape, dtype) for shape, dtype in outs],
        in_specs=[scalar if arg.ndim == 1 else vector for arg in args],
        out_specs=[vector] * len(outs),
        scratch_shapes=list(scratch),
        compiler_params=PARAMS,
    )(*args)


def place():
    at = lax.axis_index("sweep")
    return at % ROW, at // ROW


def split(value):
    high = value.astype(BF16)
    return high, (value - high.astype(F32)).astype(BF16)


def times(rows, high, low, dims):
    rows_high, rows_low = split(rows)
    count = rows.shape[0]
    both = lax.dot_general(
        jnp.concatenate([rows_high, rows_low], axis=0), high, dims, preferred_element_type=F32
    )
    cross = lax.dot_general(rows_high, low, dims, preferred_element_type=F32)
    return both[:count] + (both[count:] + cross)


def spread_body(coeff, table, source, response, before, after, sky, classes, blocked, f0, f1, f2, f3, s0, s1, s2, s3, sky_rays):
    x, y = place()
    upsun = y < 2
    density = jnp.zeros((1, K), F32)
    for at in range(table.shape[0]):
        density = jnp.where(classes[...] == at, table[at], density)
    transmit = (1 - blocked[...]).astype(F32) * jnp.exp(-coeff[0] * density)
    scale = 1.0 / math.sqrt(R)
    for dist, (first, second) in enumerate(((f0, s0), (f1, s1), (f2, s2), (f3, s3))):
        cols = pl.ds(pl.multiple_of((x + dist) % ROW * CH, CH), CH)
        weights = response[:, cols]
        up = jnp.concatenate([before[:, cols], weights[:-FV]], axis=0)
        down = jnp.concatenate([weights[FV:], after[:, cols]], axis=0)
        cotangent = ((0.5 * weights + 0.25 * (up + down)) * scale).T
        emitted = source[:, cols].T
        first[:CH] = jnp.where(upsun, emitted, cotangent)
        first[CH:] = jnp.broadcast_to(transmit, (SPARE, K))
        second[...] = jnp.where(upsun, cotangent, emitted)
    sky_rays[...] = sky[:, pl.ds(pl.multiple_of(x * CH, CH), CH)].T


def forward_chain(apply, thin, emitted, incoming, keep, first=0):
    def step(j, state):
        gained = apply(state, j, NT) * thin[j]
        state = gained + emitted[j]
        keep(j, gained, state)
        return state

    return lax.fori_loop(first, ROW, step, incoming)


def backward_chain(apply, thin, cotangent, incoming, keep, through):
    def step(i, state):
        j = ROW - 1 - i
        adjoint = cotangent[j] + state
        keep(j, adjoint)
        return apply(adjoint * thin[j], j, NN)

    state = lax.fori_loop(0, ROW - 1, step, incoming)
    adjoint = cotangent[0] + state
    keep(0, adjoint)
    if through:
        return apply(adjoint * thin[0], 0, NN)
    return None


def cut_body(left, right, e1, e2, e3, far_top, far_bottom):
    far_top[...] = left[:K // 2]
    far_bottom[...] = right[K // 2:]


def near_body(own, left, right, e0, e1, e2, e3, high, low, thin, given, pair_high, pair_low):
    x, y = place()
    for dist, part in enumerate((e0, e1, e2, e3)):
        tile = (x - dist + ROW) % ROW
        given[tile] = part[:CH]
        thin[tile] = part[CH:CH + 1]
    for dist, part in ((0, own), (1, left), (3, right)):
        tile = (x - dist + ROW) % ROW
        high[tile], low[tile] = split(part[...])

    @pl.when((y == 1) | (y == 2))
    def _():
        base = jnp.where(x < 2, 0, 2)
        rows = (high[base + 1].astype(F32) + low[base + 1].astype(F32)) * thin[base]
        pair_high[...], pair_low[...] = split(times(rows, high[base], low[base], NN))


def start_body(high, low, far_top, far_bottom, thin, given, pair_high, pair_low, sky_rays,
               far_high, far_low, saved, radiance, whole_high, whole_low, out, far_pair):
    x, y = place()
    far = (x + 2) % ROW
    far_high[:K // 2], far_low[:K // 2] = split(far_top[...])
    far_high[K // 2:], far_low[K // 2:] = split(far_bottom[...])

    def apply(rows, j, dims):
        return lax.cond(
            j == far,
            lambda: times(rows, far_high[...], far_low[...], dims),
            lambda: times(rows, high[j], low[j], dims),
        )

    @pl.when(y == 0)
    def _():
        def keep(j, gained, state):
            saved[j] = gained
            radiance[j] = state

        out[...] = forward_chain(apply, thin, given, sky_rays[...], keep)

    @pl.when(y == ROWS - 1)
    def _():
        def keep(j, adjoint):
            saved[j] = adjoint

        out[...] = backward_chain(apply, thin, given, jnp.zeros((CH, K), F32), keep, True)

    inner = (y == 1) | (y == 2)

    @pl.when(inner & (x % 2 == 0))
    def _():
        rows = (high[far + 1].astype(F32) + low[far + 1].astype(F32)) * thin[far]
        far_pair[...] = times(rows, far_high[...], far_low[...], NN)

    @pl.when(inner & (x % 2 == 1))
    def _():
        rows = (far_high[...].astype(F32) + far_low[...].astype(F32)) * thin[far - 1]
        far_pair[...] = times(rows, high[far - 1], low[far - 1], NN)

    @pl.when(inner & (x < 2))
    def _():
        whole = times(far_pair[...] * thin[1], pair_high[...], pair_low[...], NN)
        whole_high[...], whole_low[...] = split(whole)

    @pl.when(inner & (x >= 2))
    def _():
        rows = (pair_high[...].astype(F32) + pair_low[...].astype(F32)) * thin[1]
        first_high, first_low = split(far_pair[...])
        whole_high[...], whole_low[...] = split(times(rows, first_high, first_low, NN))


def held_at(high, low):
    return lambda rows, j, dims: times(rows, high[j], low[j], dims)


def ends(high, low, thin, given, y, forward_row, out):
    @pl.when(y == forward_row)
    def _():
        out[...] = forward_chain(held_at(high, low), thin, given, given[0], lambda j, g, s: None, 1)

    @pl.when(y == ROWS - 1 - forward_row)
    def _():
        out[...] = backward_chain(held_at(high, low), thin, given, jnp.zeros((CH, K), F32), lambda j, a: None, True)


def ends_body(near_high, near_low, far_high, far_low, thin, given, high, low, added):
    far = (place()[0] + 2) % ROW
    for j in range(ROW):
        @pl.when(j == far)
        def _():
            high[j] = far_high[...]
            low[j] = far_low[...]

        @pl.when(j != far)
        def _():
            high[j] = near_high[j]
            low[j] = near_low[j]

    ends(high, low, thin, given, place()[1], 1, added)


def later_body(high, low, thin, s0, s1, s2, s3, given, added):
    x, y = place()
    for dist, part in enumerate((s0, s1, s2, s3)):
        given[(x - dist + ROW) % ROW] = part[...]
    ends(high, low, thin, given, y, 2, added)


def pass_body(forward_row, incoming, whole_high, whole_low, thin, added, out):
    _, y = place()

    @pl.when(y == forward_row)
    def _():
        out[...] = times(incoming[...], whole_high[...], whole_low[...], NT) * thin[ROW - 1] + added[...]

    @pl.when(y == ROWS - 1 - forward_row)
    def _():
        out[...] = times(incoming[...] * thin[ROW - 1], whole_high[...], whole_low[...], NN) + added[...]


def middle_body(high, low, thin, given, later, first_in, second_in, radiance, along, saved):
    _, y = place()
    for row, emitted, cotangent, state, adjoint_in in (
        (1, given, later, first_in, second_in),
        (2, later, given, second_in, first_in),
    ):
        @pl.when(y == row)
        def _():
            def keep_state(j, gained, new_state):
                saved[j] = gained
                radiance[j] = new_state

            def keep_adjoint(j, adjoint):
                along[j] = jnp.sum(adjoint * saved[j], axis=0, keepdims=True)

            forward_chain(held_at(high, low), thin, emitted, state[...], keep_state)
            backward_chain(held_at(high, low), thin, cotangent, adjoint_in[...], keep_adjoint, False)


def last_body(high, low, thin, later, last_in, early, middle, gain, x0, x1, x2, x3, held):
    x, y = place()
    outs = (x0, x1, x2, x3)

    @pl.when(y == ROWS - 1)
    def _():
        def keep(j, gained, state):
            gain[j] = gained
            held[j] = state

        forward_chain(held_at(high, low), thin, later, last_in[...], keep)
        for dist, out in enumerate(outs):
            out[...] = held[(x + dist) % ROW]

    @pl.when(y == 0)
    def _():
        for dist, out in enumerate(outs):
            out[...] = early[(x + dist) % ROW]

    @pl.when((y == 1) | (y == 2))
    def _():
        for dist, out in enumerate(outs):
            out[...] = middle[(x + dist) % ROW]


def along_body(coeff, high, low, thin, later, last_in, saved, gain, middle_along, out, along):
    x, y = place()
    factor = -coeff[0]

    @pl.when(y == 0)
    def _():
        def keep(j, adjoint):
            along[j] = jnp.sum(adjoint * saved[j], axis=0, keepdims=True)

        backward_chain(held_at(high, low), thin, later, last_in[...], keep, False)

    @pl.when(y == ROWS - 1)
    def _():
        for j in range(ROW):
            along[j] = jnp.sum(gain[j] * saved[j], axis=0, keepdims=True)

    @pl.when((y == 1) | (y == 2))
    def _():
        for j in range(ROW):
            along[j] = middle_along[j]

    for j in range(ROW):
        out[j * BANDS:(j + 1) * BANDS] = jnp.broadcast_to((factor * along[j])[None], (BANDS, 1, K))


def rim_body(r0, r1, r2, r3, edge):
    x, _ = place()
    low_side = lax.axis_index("cross") == 0
    for dist, part in enumerate((r0, r1, r2, r3)):
        cols = pl.ds(pl.multiple_of((x - dist + ROW) % ROW * CH, CH), CH)
        edge[:, cols] = jnp.where(low_side, part[:, K - FV:], part[:, :FV]).T


def turn_body(r0, r1, r2, r3, out):
    x, _ = place()
    for dist, part in enumerate((r0, r1, r2, r3)):
        cols = pl.ds(pl.multiple_of((x - dist + ROW) % ROW * CH, CH), CH)
        out[:, cols] = part[...].T


def smooth_body(grid, edge, out, done):
    low_side = lax.axis_index("cross") == 0
    whole = grid[...]
    halo = edge[...]
    up = jnp.concatenate([jnp.where(low_side, 0.0, halo), whole[:-FV]], axis=0)
    down = jnp.concatenate([whole[FV:], jnp.where(low_side, halo, 0.0)], axis=0)
    out[...] = 0.5 * whole + 0.25 * (up + down)
    done[...] = halo[:8, :128]


def total_body(lines, done, out):
    out[...] = jnp.sum(lines[...], axis=0)


def per_device(operator, source, sky, response, extinction, leaf_density, leaf_class, occupied):
    local = operator[0, 0]
    weights = response[0, 0]
    side = lax.axis_index("cross")
    other_side = [(0, 1), (1, 0)]

    left = shift_x(local, 1)
    right = shift_x(local, -1)

    edge = lax.ppermute(jnp.where(side == 0, weights[-FV:], weights[:FV]), "cross", other_side)
    before = jnp.where(side == 1, edge, 0.0)
    after = jnp.where(side == 0, edge, 0.0)
    part = ((CH, K), F32)
    chunk = ((ROW, CH, K), F32)
    line = ((ROW, 1, K), F32)
    first = ((CH + SPARE, K), F32)
    f0, f1, f2, f3, s0, s1, s2, s3, sky_rays = call(
        spread_body, [first] * ROW + [part] * (ROW + 1),
        extinction, leaf_density, source[0, 0], weights, before, after, sky[0], leaf_class, occupied)
    e0, e1, e2, e3 = f0, shift_x(f1, 1), shift_x(f2, 2), shift_x(f3, 3)
    half = ((K // 2, K), F32)
    operators = ((ROW, K, K), BF16)
    whole = ((K, K), BF16)
    far_top, far_bottom = call(cut_body, [half, half], left, right, e1, e2, e3)
    far_top = shift_x(far_top, 1)
    far_bottom = shift_x(far_bottom, -1)
    near_high, near_low, thin, given, pair_high, pair_low = call(
        near_body, [operators, operators, line, chunk, whole, whole], local, left, right, e0, e1, e2, e3)
    far_high, far_low, saved, early, whole_high, whole_low, out = call(
        start_body, [whole, whole, chunk, chunk, whole, whole, part],
        near_high, near_low, far_top, far_bottom, thin, given, pair_high, pair_low, sky_rays,
        scratch=[pltpu.VMEM((K, K), F32)])
    first_in = lax.ppermute(out, "sweep", Y_SWAP)
    s1, s2, s3 = shift_x(s1, 1), shift_x(s2, 2), shift_x(s3, 3)
    high, low, added = call(
        ends_body, [operators, operators, part], near_high, near_low, far_high, far_low, thin, given)
    (out,) = call(functools.partial(pass_body, 1), [part], first_in, whole_high, whole_low, thin, added)
    second_in = lax.ppermute(out, "sweep", Y_TURN)
    later, added = call(later_body, [chunk, part], high, low, thin, s0, s1, s2, s3)
    (out,) = call(functools.partial(pass_body, 2), [part], second_in, whole_high, whole_low, thin, added)
    last_in = lax.ppermute(out, "sweep", Y_SWAP)
    held = pltpu.VMEM((ROW, CH, K), F32)
    middle, middle_along = call(
        middle_body, [chunk, line], high, low, thin, given, later, first_in, second_in, scratch=[held])
    gain, x0, x1, x2, x3 = call(
        last_body, [chunk] + [part] * ROW, high, low, thin, later, last_in, early, middle, scratch=[held])
    r0, r1, r2, r3 = x0, shift_x(x1, 1), shift_x(x2, 2), shift_x(x3, 3)
    (lines,) = call(
        along_body, [((ROW * BANDS, 1, K), F32)], extinction, high, low, thin, later, last_in, saved, gain, middle_along,
        scratch=[pltpu.VMEM((ROW, 1, K), F32)])
    lines = lax.all_to_all(lines, ("sweep", "band"), 0, 0, axis_index_groups=ROW_BANDS)

    (edge,) = call(rim_body, [((FV, R), F32)], r0, r1, r2, r3)
    edge = lax.ppermute(edge, "cross", other_side)
    (grid,) = call(turn_body, [((K, R), F32)], r0, r1, r2, r3)
    observed, done = call(smooth_body, [((K, R), F32), ((8, 128), F32)], grid, edge)
    (total,) = call(total_body, [((1, K), F32)], lines, done)
    return (observed[None, None], total)


def solution(mesh):
    in_specs = (
        P("band", "sweep", "cross", None),
        P("band", "sweep", "cross", None),
        P("band", "cross", None),
        P("band", "sweep", "cross", None),
        P("band"),
        P(),
        P("sweep", "cross"),
        P("sweep", "cross"),
    )
    out_specs = (P("band", "sweep", "cross", None), P("sweep", "cross"))
    return jax.shard_map(
        per_device, mesh=mesh, in_specs=in_specs, out_specs=out_specs, check_vma=False
    )
```

```python
import functools
import math

import jax
import jax.numpy as jnp
from jax import lax
from jax.experimental import pallas as pl
from jax.experimental.pallas import tpu as pltpu
from jax.sharding import PartitionSpec as P

K = 512
R = 512
FV = 32
ROW = 4
ROWS = 4
CH = R // ROW
BANDS = 8
SPARE = 8
F32 = jnp.float32
BF16 = jnp.bfloat16
NT = (((1,), (1,)), ((), ()))
NN = (((1,), (0,)), ((), ()))
PARAMS = pltpu.CompilerParams(vmem_limit_bytes=24 * 1024 * 1024)

X_RING = {
    d: [(ROW * y + x, ROW * y + (x + d) % ROW) for y in range(ROWS) for x in range(ROW)] for d in range(1, ROW)
}
SWAP = [1, 0, 3, 2]
TURN = [3, 2, 1, 0]
Y_SWAP = [(ROW * y + x, ROW * SWAP[y] + x) for y in range(ROWS) for x in range(ROW)]
Y_TURN = [(ROW * y + x, ROW * TURN[y] + x) for y in range(ROWS) for x in range(ROW)]
ROW_BANDS = [[(ROW * y + x) * BANDS + z for x in range(ROW) for z in range(BANDS)] for y in range(ROWS)]


def shift_x(value, by):
    return lax.ppermute(value, "sweep", X_RING[by % ROW])


def call(body, outs, *args, scratch=()):
    scalar = pl.BlockSpec(memory_space=pltpu.SMEM)
    vector = pl.BlockSpec(memory_space=pltpu.VMEM)
    return pl.pallas_call(
        body,
        out_shape=[jax.ShapeDtypeStruct(shape, dtype) for shape, dtype in outs],
        in_specs=[scalar if arg.ndim == 1 else vector for arg in args],
        out_specs=[vector] * len(outs),
        scratch_shapes=list(scratch),
        compiler_params=PARAMS,
    )(*args)


def place():
    at = lax.axis_index("sweep")
    return at % ROW, at // ROW


def split(value):
    high = value.astype(BF16)
    return high, (value - high.astype(F32)).astype(BF16)


def times(rows, high, low, dims):
    rows_high, rows_low = split(rows)
    count = rows.shape[0]
    both = lax.dot_general(
        jnp.concatenate([rows_high, rows_low], axis=0), high, dims, preferred_element_type=F32
    )
    cross = lax.dot_general(rows_high, low, dims, preferred_element_type=F32)
    return both[:count] + (both[count:] + cross)


def spread_body(coeff, table, source, response, before, after, sky, classes, blocked, f0, f1, f2, f3, s0, s1, s2, s3, sky_rays):
    x, y = place()
    upsun = y < 2
    density = jnp.zeros((1, K), F32)
    for at in range(table.shape[0]):
        density = jnp.where(classes[...] == at, table[at], density)
    transmit = (1 - blocked[...]).astype(F32) * jnp.exp(-coeff[0] * density)
    scale = 1.0 / math.sqrt(R)
    for dist, (first, second) in enumerate(((f0, s0), (f1, s1), (f2, s2), (f3, s3))):
        cols = pl.ds(pl.multiple_of((x + dist) % ROW * CH, CH), CH)
        weights = response[:, cols]
        up = jnp.concatenate([before[:, cols], weights[:-FV]], axis=0)
        down = jnp.concatenate([weights[FV:], after[:, cols]], axis=0)
        cotangent = ((0.5 * weights + 0.25 * (up + down)) * scale).T
        emitted = source[:, cols].T
        first[:CH] = jnp.where(upsun, emitted, cotangent)
        first[CH:] = jnp.broadcast_to(transmit, (SPARE, K))
        second[...] = jnp.where(upsun, cotangent, emitted)
    sky_rays[...] = sky[:, pl.ds(pl.multiple_of(x * CH, CH), CH)].T


def forward_chain(apply, thin, emitted, incoming, keep, first=0):
    def step(j, state):
        gained = apply(state, j, NT) * thin[j]
        state = gained + emitted[j]
        keep(j, gained, state)
        return state

    return lax.fori_loop(first, ROW, step, incoming, unroll=True)


def backward_chain(apply, thin, cotangent, incoming, keep, through):
    def step(i, state):
        j = ROW - 1 - i
        adjoint = cotangent[j] + state
        keep(j, adjoint)
        return apply(adjoint * thin[j], j, NN)

    state = lax.fori_loop(0, ROW - 1, step, incoming, unroll=True)
    adjoint = cotangent[0] + state
    keep(0, adjoint)
    if through:
        return apply(adjoint * thin[0], 0, NN)
    return None


def cut_body(left, right, e1, e2, e3, far_top, far_bottom):
    far_top[...] = left[:K // 2]
    far_bottom[...] = right[K // 2:]


def near_body(own, left, right, e0, e1, e2, e3, high, low, thin, given, pair_high, pair_low):
    x, y = place()
    for dist, part in enumerate((e0, e1, e2, e3)):
        tile = (x - dist + ROW) % ROW
        given[tile] = part[:CH]
        thin[tile] = part[CH:CH + 1]
    for dist, part in ((0, own), (1, left), (3, right)):
        tile = (x - dist + ROW) % ROW
        high[tile], low[tile] = split(part[...])

    @pl.when((y == 1) | (y == 2))
    def _():
        base = jnp.where(x < 2, 0, 2)
        rows = (high[base + 1].astype(F32) + low[base + 1].astype(F32)) * thin[base]
        pair_high[...], pair_low[...] = split(times(rows, high[base], low[base], NN))


def start_body(high, low, far_top, far_bottom, thin, given, pair_high, pair_low, sky_rays,
               far_high, far_low, saved, radiance, whole_high, whole_low, out, far_pair):
    x, y = place()
    far = (x + 2) % ROW
    far_high[:K // 2], far_low[:K // 2] = split(far_top[...])
    far_high[K // 2:], far_low[K // 2:] = split(far_bottom[...])

    def apply(rows, j, dims):
        return lax.cond(
            j == far,
            lambda: times(rows, far_high[...], far_low[...], dims),
            lambda: times(rows, high[j], low[j], dims),
        )

    @pl.when(y == 0)
    def _():
        def keep(j, gained, state):
            saved[j] = gained
            radiance[j] = state

        out[...] = forward_chain(apply, thin, given, sky_rays[...], keep)

    @pl.when(y == ROWS - 1)
    def _():
        def keep(j, adjoint):
            saved[j] = adjoint

        out[...] = backward_chain(apply, thin, given, jnp.zeros((CH, K), F32), keep, True)

    inner = (y == 1) | (y == 2)

    @pl.when(inner & (x % 2 == 0))
    def _():
        rows = (high[far + 1].astype(F32) + low[far + 1].astype(F32)) * thin[far]
        far_pair[...] = times(rows, far_high[...], far_low[...], NN)

    @pl.when(inner & (x % 2 == 1))
    def _():
        rows = (far_high[...].astype(F32) + far_low[...].astype(F32)) * thin[far - 1]
        far_pair[...] = times(rows, high[far - 1], low[far - 1], NN)

    @pl.when(inner & (x < 2))
    def _():
        whole = times(far_pair[...] * thin[1], pair_high[...], pair_low[...], NN)
        whole_high[...], whole_low[...] = split(whole)

    @pl.when(inner & (x >= 2))
    def _():
        rows = (pair_high[...].astype(F32) + pair_low[...].astype(F32)) * thin[1]
        first_high, first_low = split(far_pair[...])
        whole_high[...], whole_low[...] = split(times(rows, first_high, first_low, NN))


def held_at(high, low):
    return lambda rows, j, dims: times(rows, high[j], low[j], dims)


def ends(high, low, thin, given, y, forward_row, out):
    @pl.when(y == forward_row)
    def _():
        out[...] = forward_chain(held_at(high, low), thin, given, given[0], lambda j, g, s: None, 1)

    @pl.when(y == ROWS - 1 - forward_row)
    def _():
        out[...] = backward_chain(held_at(high, low), thin, given, jnp.zeros((CH, K), F32), lambda j, a: None, True)


def ends_body(near_high, near_low, far_high, far_low, thin, given, high, low, added):
    far = (place()[0] + 2) % ROW
    for j in range(ROW):
        @pl.when(j == far)
        def _():
            high[j] = far_high[...]
            low[j] = far_low[...]

        @pl.when(j != far)
        def _():
            high[j] = near_high[j]
            low[j] = near_low[j]

    ends(high, low, thin, given, place()[1], 1, added)


def later_body(high, low, thin, s0, s1, s2, s3, given, added):
    x, y = place()
    for dist, part in enumerate((s0, s1, s2, s3)):
        given[(x - dist + ROW) % ROW] = part[...]
    ends(high, low, thin, given, y, 2, added)


def pass_body(forward_row, incoming, whole_high, whole_low, thin, added, out):
    _, y = place()

    @pl.when(y == forward_row)
    def _():
        out[...] = times(incoming[...], whole_high[...], whole_low[...], NT) * thin[ROW - 1] + added[...]

    @pl.when(y == ROWS - 1 - forward_row)
    def _():
        out[...] = times(incoming[...] * thin[ROW - 1], whole_high[...], whole_low[...], NN) + added[...]


def middle_body(high, low, thin, given, later, first_in, second_in, radiance, along, saved):
    _, y = place()
    for row, emitted, cotangent, state, adjoint_in in (
        (1, given, later, first_in, second_in),
        (2, later, given, second_in, first_in),
    ):
        @pl.when(y == row)
        def _():
            def keep_state(j, gained, new_state):
                saved[j] = gained
                radiance[j] = new_state

            def keep_adjoint(j, adjoint):
                along[j] = jnp.sum(adjoint * saved[j], axis=0, keepdims=True)

            forward_chain(held_at(high, low), thin, emitted, state[...], keep_state)
            backward_chain(held_at(high, low), thin, cotangent, adjoint_in[...], keep_adjoint, False)


def last_body(high, low, thin, later, last_in, early, middle, gain, x0, x1, x2, x3, held):
    x, y = place()
    outs = (x0, x1, x2, x3)

    @pl.when(y == ROWS - 1)
    def _():
        def keep(j, gained, state):
            gain[j] = gained
            held[j] = state

        forward_chain(held_at(high, low), thin, later, last_in[...], keep)
        for dist, out in enumerate(outs):
            out[...] = held[(x + dist) % ROW]

    @pl.when(y == 0)
    def _():
        for dist, out in enumerate(outs):
            out[...] = early[(x + dist) % ROW]

    @pl.when((y == 1) | (y == 2))
    def _():
        for dist, out in enumerate(outs):
            out[...] = middle[(x + dist) % ROW]


def along_body(coeff, high, low, thin, later, last_in, saved, gain, middle_along, out, along):
    x, y = place()
    factor = -coeff[0]

    @pl.when(y == 0)
    def _():
        def keep(j, adjoint):
            along[j] = jnp.sum(adjoint * saved[j], axis=0, keepdims=True)

        backward_chain(held_at(high, low), thin, later, last_in[...], keep, False)

    @pl.when(y == ROWS - 1)
    def _():
        for j in range(ROW):
            along[j] = jnp.sum(gain[j] * saved[j], axis=0, keepdims=True)

    @pl.when((y == 1) | (y == 2))
    def _():
        for j in range(ROW):
            along[j] = middle_along[j]

    for j in range(ROW):
        out[j * BANDS:(j + 1) * BANDS] = jnp.broadcast_to((factor * along[j])[None], (BANDS, 1, K))


def rim_body(r0, r1, r2, r3, edge):
    x, _ = place()
    low_side = lax.axis_index("cross") == 0
    for dist, part in enumerate((r0, r1, r2, r3)):
        cols = pl.ds(pl.multiple_of((x - dist + ROW) % ROW * CH, CH), CH)
        edge[:, cols] = jnp.where(low_side, part[:, K - FV:], part[:, :FV]).T


def turn_body(r0, r1, r2, r3, out):
    x, _ = place()
    for dist, part in enumerate((r0, r1, r2, r3)):
        cols = pl.ds(pl.multiple_of((x - dist + ROW) % ROW * CH, CH), CH)
        out[:, cols] = part[...].T


def smooth_body(grid, edge, out, done):
    low_side = lax.axis_index("cross") == 0
    whole = grid[...]
    halo = edge[...]
    up = jnp.concatenate([jnp.where(low_side, 0.0, halo), whole[:-FV]], axis=0)
    down = jnp.concatenate([whole[FV:], jnp.where(low_side, halo, 0.0)], axis=0)
    out[...] = 0.5 * whole + 0.25 * (up + down)
    done[...] = halo[:8, :128]


def total_body(lines, done, out):
    out[...] = jnp.sum(lines[...], axis=0)


def per_device(operator, source, sky, response, extinction, leaf_density, leaf_class, occupied):
    local = operator[0, 0]
    weights = response[0, 0]
    side = lax.axis_index("cross")
    other_side = [(0, 1), (1, 0)]

    left = shift_x(local, 1)
    right = shift_x(local, -1)

    edge = lax.ppermute(jnp.where(side == 0, weights[-FV:], weights[:FV]), "cross", other_side)
    before = jnp.where(side == 1, edge, 0.0)
    after = jnp.where(side == 0, edge, 0.0)
    part = ((CH, K), F32)
    chunk = ((ROW, CH, K), F32)
    line = ((ROW, 1, K), F32)
    first = ((CH + SPARE, K), F32)
    f0, f1, f2, f3, s0, s1, s2, s3, sky_rays = call(
        spread_body, [first] * ROW + [part] * (ROW + 1),
        extinction, leaf_density, source[0, 0], weights, before, after, sky[0], leaf_class, occupied)
    e0, e1, e2, e3 = f0, shift_x(f1, 1), shift_x(f2, 2), shift_x(f3, 3)
    half = ((K // 2, K), F32)
    operators = ((ROW, K, K), BF16)
    whole = ((K, K), BF16)
    far_top, far_bottom = call(cut_body, [half, half], left, right, e1, e2, e3)
    far_top = shift_x(far_top, 1)
    far_bottom = shift_x(far_bottom, -1)
    near_high, near_low, thin, given, pair_high, pair_low = call(
        near_body, [operators, operators, line, chunk, whole, whole], local, left, right, e0, e1, e2, e3)
    far_high, far_low, saved, early, whole_high, whole_low, out = call(
        start_body, [whole, whole, chunk, chunk, whole, whole, part],
        near_high, near_low, far_top, far_bottom, thin, given, pair_high, pair_low, sky_rays,
        scratch=[pltpu.VMEM((K, K), F32)])
    first_in = lax.ppermute(out, "sweep", Y_SWAP)
    s1, s2, s3 = shift_x(s1, 1), shift_x(s2, 2), shift_x(s3, 3)
    high, low, added = call(
        ends_body, [operators, operators, part], near_high, near_low, far_high, far_low, thin, given)
    (out,) = call(functools.partial(pass_body, 1), [part], first_in, whole_high, whole_low, thin, added)
    second_in = lax.ppermute(out, "sweep", Y_TURN)
    later, added = call(later_body, [chunk, part], high, low, thin, s0, s1, s2, s3)
    (out,) = call(functools.partial(pass_body, 2), [part], second_in, whole_high, whole_low, thin, added)
    last_in = lax.ppermute(out, "sweep", Y_SWAP)
    held = pltpu.VMEM((ROW, CH, K), F32)
    middle, middle_along = call(
        middle_body, [chunk, line], high, low, thin, given, later, first_in, second_in, scratch=[held])
    gain, x0, x1, x2, x3 = call(
        last_body, [chunk] + [part] * ROW, high, low, thin, later, last_in, early, middle, scratch=[held])
    r0, r1, r2, r3 = x0, shift_x(x1, 1), shift_x(x2, 2), shift_x(x3, 3)
    (lines,) = call(
        along_body, [((ROW * BANDS, 1, K), F32)], extinction, high, low, thin, later, last_in, saved, gain, middle_along,
        scratch=[pltpu.VMEM((ROW, 1, K), F32)])
    lines = lax.all_to_all(lines, ("sweep", "band"), 0, 0, axis_index_groups=ROW_BANDS)

    (edge,) = call(rim_body, [((FV, R), F32)], r0, r1, r2, r3)
    edge = lax.ppermute(edge, "cross", other_side)
    (grid,) = call(turn_body, [((K, R), F32)], r0, r1, r2, r3)
    observed, done = call(smooth_body, [((K, R), F32), ((8, 128), F32)], grid, edge)
    (total,) = call(total_body, [((1, K), F32)], lines, done)
    return (observed[None, None], total)


def solution(mesh):
    in_specs = (
        P("band", "sweep", "cross", None),
        P("band", "sweep", "cross", None),
        P("band", "cross", None),
        P("band", "sweep", "cross", None),
        P("band"),
        P(),
        P("sweep", "cross"),
        P("sweep", "cross"),
    )
    out_specs = (P("band", "sweep", "cross", None), P("sweep", "cross"))
    return jax.shard_map(
        per_device, mesh=mesh, in_specs=in_specs, out_specs=out_specs, check_vma=False
    )
```

```python
import functools
import math

import jax
import jax.numpy as jnp
from jax import lax
from jax.experimental import pallas as pl
from jax.experimental.pallas import tpu as pltpu
from jax.sharding import PartitionSpec as P

K = 512
R = 512
FV = 32
ROW = 4
ROWS = 4
CH = R // ROW
BANDS = 8
SPARE = 8
F32 = jnp.float32
BF16 = jnp.bfloat16
NT = (((1,), (1,)), ((), ()))
NN = (((1,), (0,)), ((), ()))
PARAMS = pltpu.CompilerParams(vmem_limit_bytes=18 * 1024 * 1024)

X_RING = {
    d: [(ROW * y + x, ROW * y + (x + d) % ROW) for y in range(ROWS) for x in range(ROW)] for d in range(1, ROW)
}
SWAP = [1, 0, 3, 2]
TURN = [3, 2, 1, 0]
Y_SWAP = [(ROW * y + x, ROW * SWAP[y] + x) for y in range(ROWS) for x in range(ROW)]
Y_TURN = [(ROW * y + x, ROW * TURN[y] + x) for y in range(ROWS) for x in range(ROW)]
ROW_BANDS = [[(ROW * y + x) * BANDS + z for x in range(ROW) for z in range(BANDS)] for y in range(ROWS)]


def shift_x(value, by):
    return lax.ppermute(value, "sweep", X_RING[by % ROW])


def call(body, outs, *args, scratch=()):
    scalar = pl.BlockSpec(memory_space=pltpu.SMEM)
    vector = pl.BlockSpec(memory_space=pltpu.VMEM)
    return pl.pallas_call(
        body,
        out_shape=[jax.ShapeDtypeStruct(shape, dtype) for shape, dtype in outs],
        in_specs=[scalar if arg.ndim == 1 else vector for arg in args],
        out_specs=[vector] * len(outs),
        scratch_shapes=list(scratch),
        compiler_params=PARAMS,
    )(*args)


def place():
    at = lax.axis_index("sweep")
    return at % ROW, at // ROW


def split(value):
    high = value.astype(BF16)
    return high, (value - high.astype(F32)).astype(BF16)


def times(rows, high, low, dims):
    rows_high, rows_low = split(rows)
    count = rows.shape[0]
    both = lax.dot_general(
        jnp.concatenate([rows_high, rows_low], axis=0), high, dims, preferred_element_type=F32
    )
    cross = lax.dot_general(rows_high, low, dims, preferred_element_type=F32)
    return both[:count] + (both[count:] + cross)


def spread_body(coeff, table, source, response, before, after, sky, classes, blocked, f0, f1, f2, f3, s0, s1, s2, s3, sky_rays):
    x, y = place()
    upsun = y < 2
    density = jnp.zeros((1, K), F32)
    for at in range(table.shape[0]):
        density = jnp.where(classes[...] == at, table[at], density)
    transmit = (1 - blocked[...]).astype(F32) * jnp.exp(-coeff[0] * density)
    scale = 1.0 / math.sqrt(R)
    for dist, (first, second) in enumerate(((f0, s0), (f1, s1), (f2, s2), (f3, s3))):
        cols = pl.ds(pl.multiple_of((x + dist) % ROW * CH, CH), CH)
        weights = response[:, cols]
        up = jnp.concatenate([before[:, cols], weights[:-FV]], axis=0)
        down = jnp.concatenate([weights[FV:], after[:, cols]], axis=0)
        cotangent = ((0.5 * weights + 0.25 * (up + down)) * scale).T
        emitted = source[:, cols].T
        first[:CH] = jnp.where(upsun, emitted, cotangent)
        first[CH:] = jnp.broadcast_to(transmit, (SPARE, K))
        second[...] = jnp.where(upsun, cotangent, emitted)
    sky_rays[...] = sky[:, pl.ds(pl.multiple_of(x * CH, CH), CH)].T


def forward_chain(apply, thin, emitted, incoming, keep, first=0):
    def step(j, state):
        gained = apply(state, j, NT) * thin[j]
        state = gained + emitted[j]
        keep(j, gained, state)
        return state

    return lax.fori_loop(first, ROW, step, incoming, unroll=True)


def backward_chain(apply, thin, cotangent, incoming, keep, through):
    def step(i, state):
        j = ROW - 1 - i
        adjoint = cotangent[j] + state
        keep(j, adjoint)
        return apply(adjoint * thin[j], j, NN)

    state = lax.fori_loop(0, ROW - 1, step, incoming, unroll=True)
    adjoint = cotangent[0] + state
    keep(0, adjoint)
    if through:
        return apply(adjoint * thin[0], 0, NN)
    return None


def cut_body(left, right, e1, e2, e3, far_top, far_bottom):
    far_top[...] = left[:K // 2]
    far_bottom[...] = right[K // 2:]


def near_body(own, left, right, e0, e1, e2, e3, high, low, thin, given, pair_high, pair_low):
    x, y = place()
    for dist, part in enumerate((e0, e1, e2, e3)):
        tile = (x - dist + ROW) % ROW
        given[tile] = part[:CH]
        thin[tile] = part[CH:CH + 1]
    for dist, part in ((0, own), (1, left), (3, right)):
        tile = (x - dist + ROW) % ROW
        high[tile], low[tile] = split(part[...])

    @pl.when((y == 1) | (y == 2))
    def _():
        base = jnp.where(x < 2, 0, 2)
        rows = (high[base + 1].astype(F32) + low[base + 1].astype(F32)) * thin[base]
        pair_high[...], pair_low[...] = split(times(rows, high[base], low[base], NN))


def start_body(high, low, far_top, far_bottom, thin, given, pair_high, pair_low, sky_rays,
               far_high, far_low, saved, radiance, whole_high, whole_low, out, far_pair):
    x, y = place()
    far = (x + 2) % ROW
    far_high[:K // 2], far_low[:K // 2] = split(far_top[...])
    far_high[K // 2:], far_low[K // 2:] = split(far_bottom[...])

    def apply(rows, j, dims):
        return lax.cond(
            j == far,
            lambda: times(rows, far_high[...], far_low[...], dims),
            lambda: times(rows, high[j], low[j], dims),
        )

    @pl.when(y == 0)
    def _():
        def keep(j, gained, state):
            saved[j] = gained
            radiance[j] = state

        out[...] = forward_chain(apply, thin, given, sky_rays[...], keep)

    @pl.when(y == ROWS - 1)
    def _():
        def keep(j, adjoint):
            saved[j] = adjoint

        out[...] = backward_chain(apply, thin, given, jnp.zeros((CH, K), F32), keep, True)

    inner = (y == 1) | (y == 2)

    @pl.when(inner & (x % 2 == 0))
    def _():
        rows = (high[far + 1].astype(F32) + low[far + 1].astype(F32)) * thin[far]
        far_pair[...] = times(rows, far_high[...], far_low[...], NN)

    @pl.when(inner & (x % 2 == 1))
    def _():
        rows = (far_high[...].astype(F32) + far_low[...].astype(F32)) * thin[far - 1]
        far_pair[...] = times(rows, high[far - 1], low[far - 1], NN)

    @pl.when(inner & (x < 2))
    def _():
        whole = times(far_pair[...] * thin[1], pair_high[...], pair_low[...], NN)
        whole_high[...], whole_low[...] = split(whole)

    @pl.when(inner & (x >= 2))
    def _():
        rows = (pair_high[...].astype(F32) + pair_low[...].astype(F32)) * thin[1]
        first_high, first_low = split(far_pair[...])
        whole_high[...], whole_low[...] = split(times(rows, first_high, first_low, NN))


def held_at(high, low):
    return lambda rows, j, dims: times(rows, high[j], low[j], dims)


def ends(high, low, thin, given, y, forward_row, out):
    @pl.when(y == forward_row)
    def _():
        out[...] = forward_chain(held_at(high, low), thin, given, given[0], lambda j, g, s: None, 1)

    @pl.when(y == ROWS - 1 - forward_row)
    def _():
        out[...] = backward_chain(held_at(high, low), thin, given, jnp.zeros((CH, K), F32), lambda j, a: None, True)


def ends_body(near_high, near_low, far_high, far_low, thin, given, high, low, added):
    far = (place()[0] + 2) % ROW
    for j in range(ROW):
        @pl.when(j == far)
        def _():
            high[j] = far_high[...]
            low[j] = far_low[...]

        @pl.when(j != far)
        def _():
            high[j] = near_high[j]
            low[j] = near_low[j]

    ends(high, low, thin, given, place()[1], 1, added)


def later_body(high, low, thin, s0, s1, s2, s3, given, added):
    x, y = place()
    for dist, part in enumerate((s0, s1, s2, s3)):
        given[(x - dist + ROW) % ROW] = part[...]
    ends(high, low, thin, given, y, 2, added)


def pass_body(forward_row, incoming, whole_high, whole_low, thin, added, out):
    _, y = place()

    @pl.when(y == forward_row)
    def _():
        out[...] = times(incoming[...], whole_high[...], whole_low[...], NT) * thin[ROW - 1] + added[...]

    @pl.when(y == ROWS - 1 - forward_row)
    def _():
        out[...] = times(incoming[...] * thin[ROW - 1], whole_high[...], whole_low[...], NN) + added[...]


def middle_body(high, low, thin, given, later, first_in, second_in, radiance, along, saved):
    _, y = place()
    for row, emitted, cotangent, state, adjoint_in in (
        (1, given, later, first_in, second_in),
        (2, later, given, second_in, first_in),
    ):
        @pl.when(y == row)
        def _():
            def keep_state(j, gained, new_state):
                saved[j] = gained
                radiance[j] = new_state

            def keep_adjoint(j, adjoint):
                along[j] = jnp.sum(adjoint * saved[j], axis=0, keepdims=True)

            forward_chain(held_at(high, low), thin, emitted, state[...], keep_state)
            backward_chain(held_at(high, low), thin, cotangent, adjoint_in[...], keep_adjoint, False)


def last_body(high, low, thin, later, last_in, early, middle, gain, x0, x1, x2, x3, held):
    x, y = place()
    outs = (x0, x1, x2, x3)

    @pl.when(y == ROWS - 1)
    def _():
        def keep(j, gained, state):
            gain[j] = gained
            held[j] = state

        forward_chain(held_at(high, low), thin, later, last_in[...], keep)
        for dist, out in enumerate(outs):
            out[...] = held[(x + dist) % ROW]

    @pl.when(y == 0)
    def _():
        for dist, out in enumerate(outs):
            out[...] = early[(x + dist) % ROW]

    @pl.when((y == 1) | (y == 2))
    def _():
        for dist, out in enumerate(outs):
            out[...] = middle[(x + dist) % ROW]


def along_body(coeff, high, low, thin, later, last_in, saved, gain, middle_along, out, along):
    x, y = place()
    factor = -coeff[0]

    @pl.when(y == 0)
    def _():
        def keep(j, adjoint):
            along[j] = jnp.sum(adjoint * saved[j], axis=0, keepdims=True)

        backward_chain(held_at(high, low), thin, later, last_in[...], keep, False)

    @pl.when(y == ROWS - 1)
    def _():
        for j in range(ROW):
            along[j] = jnp.sum(gain[j] * saved[j], axis=0, keepdims=True)

    @pl.when((y == 1) | (y == 2))
    def _():
        for j in range(ROW):
            along[j] = middle_along[j]

    for j in range(ROW):
        out[j * BANDS:(j + 1) * BANDS] = jnp.broadcast_to((factor * along[j])[None], (BANDS, 1, K))


def rim_body(r0, r1, r2, r3, edge):
    x, _ = place()
    low_side = lax.axis_index("cross") == 0
    for dist, part in enumerate((r0, r1, r2, r3)):
        cols = pl.ds(pl.multiple_of((x - dist + ROW) % ROW * CH, CH), CH)
        edge[:, cols] = jnp.where(low_side, part[:, K - FV:], part[:, :FV]).T


def turn_body(r0, r1, r2, r3, out):
    x, _ = place()
    for dist, part in enumerate((r0, r1, r2, r3)):
        cols = pl.ds(pl.multiple_of((x - dist + ROW) % ROW * CH, CH), CH)
        out[:, cols] = part[...].T


def smooth_body(grid, edge, out, done):
    low_side = lax.axis_index("cross") == 0
    whole = grid[...]
    halo = edge[...]
    up = jnp.concatenate([jnp.where(low_side, 0.0, halo), whole[:-FV]], axis=0)
    down = jnp.concatenate([whole[FV:], jnp.where(low_side, halo, 0.0)], axis=0)
    out[...] = 0.5 * whole + 0.25 * (up + down)
    done[...] = halo[:8, :128]


def total_body(lines, done, out):
    out[...] = jnp.sum(lines[...], axis=0)


def per_device(operator, source, sky, response, extinction, leaf_density, leaf_class, occupied):
    local = operator[0, 0]
    weights = response[0, 0]
    side = lax.axis_index("cross")
    other_side = [(0, 1), (1, 0)]

    left = shift_x(local, 1)
    right = shift_x(local, -1)

    edge = lax.ppermute(jnp.where(side == 0, weights[-FV:], weights[:FV]), "cross", other_side)
    before = jnp.where(side == 1, edge, 0.0)
    after = jnp.where(side == 0, edge, 0.0)
    part = ((CH, K), F32)
    chunk = ((ROW, CH, K), F32)
    line = ((ROW, 1, K), F32)
    first = ((CH + SPARE, K), F32)
    f0, f1, f2, f3, s0, s1, s2, s3, sky_rays = call(
        spread_body, [first] * ROW + [part] * (ROW + 1),
        extinction, leaf_density, source[0, 0], weights, before, after, sky[0], leaf_class, occupied)
    e0 = f0
    e2 = shift_x(f2, 2)
    e3 = shift_x(f3, 3)
    e1 = shift_x(f1, 1)
    half = ((K // 2, K), F32)
    operators = ((ROW, K, K), BF16)
    whole = ((K, K), BF16)
    far_top, far_bottom = call(cut_body, [half, half], left, right, e1, e2, e3)
    far_bottom = shift_x(far_bottom, -1)
    far_top = shift_x(far_top, 1)
    near_high, near_low, thin, given, pair_high, pair_low = call(
        near_body, [operators, operators, line, chunk, whole, whole], local, left, right, e0, e1, e2, e3)
    far_high, far_low, saved, early, whole_high, whole_low, out = call(
        start_body, [whole, whole, chunk, chunk, whole, whole, part],
        near_high, near_low, far_top, far_bottom, thin, given, pair_high, pair_low, sky_rays,
        scratch=[pltpu.VMEM((K, K), F32)])
    first_in = lax.ppermute(out, "sweep", Y_SWAP)
    s1, s2, s3 = shift_x(s1, 1), shift_x(s2, 2), shift_x(s3, 3)
    high, low, added = call(
        ends_body, [operators, operators, part], near_high, near_low, far_high, far_low, thin, given)
    (out,) = call(functools.partial(pass_body, 1), [part], first_in, whole_high, whole_low, thin, added)
    second_in = lax.ppermute(out, "sweep", Y_TURN)
    later, added = call(later_body, [chunk, part], high, low, thin, s0, s1, s2, s3)
    (out,) = call(functools.partial(pass_body, 2), [part], second_in, whole_high, whole_low, thin, added)
    last_in = lax.ppermute(out, "sweep", Y_SWAP)
    held = pltpu.VMEM((ROW, CH, K), F32)
    middle, middle_along = call(
        middle_body, [chunk, line], high, low, thin, given, later, first_in, second_in, scratch=[held])
    gain, x0, x1, x2, x3 = call(
        last_body, [chunk] + [part] * ROW, high, low, thin, later, last_in, early, middle, scratch=[held])
    r0, r1, r2, r3 = x0, shift_x(x1, 1), shift_x(x2, 2), shift_x(x3, 3)
    (lines,) = call(
        along_body, [((ROW * BANDS, 1, K), F32)], extinction, high, low, thin, later, last_in, saved, gain, middle_along,
        scratch=[pltpu.VMEM((ROW, 1, K), F32)])
    lines = lax.all_to_all(lines, ("sweep", "band"), 0, 0, axis_index_groups=ROW_BANDS)

    (edge,) = call(rim_body, [((FV, R), F32)], r0, r1, r2, r3)
    edge = lax.ppermute(edge, "cross", other_side)
    (grid,) = call(turn_body, [((K, R), F32)], r0, r1, r2, r3)
    observed, done = call(smooth_body, [((K, R), F32), ((8, 128), F32)], grid, edge)
    (total,) = call(total_body, [((1, K), F32)], lines, done)
    return (observed[None, None], total)


def solution(mesh):
    in_specs = (
        P("band", "sweep", "cross", None),
        P("band", "sweep", "cross", None),
        P("band", "cross", None),
        P("band", "sweep", "cross", None),
        P("band"),
        P(),
        P("sweep", "cross"),
        P("sweep", "cross"),
    )
    out_specs = (P("band", "sweep", "cross", None), P("sweep", "cross"))
    return jax.shard_map(
        per_device, mesh=mesh, in_specs=in_specs, out_specs=out_specs, check_vma=False
    )
```

```python
import functools
import math

import jax
import jax.numpy as jnp
from jax import lax
from jax.experimental import pallas as pl
from jax.experimental.pallas import tpu as pltpu
from jax.sharding import PartitionSpec as P

K = 512
R = 512
FV = 32
ROW = 4
ROWS = 4
CH = R // ROW
BANDS = 8
SPARE = 8
F32 = jnp.float32
BF16 = jnp.bfloat16
NT = (((1,), (1,)), ((), ()))
NN = (((1,), (0,)), ((), ()))
PARAMS = pltpu.CompilerParams(vmem_limit_bytes=18 * 1024 * 1024)

X_RING = {
    d: [(ROW * y + x, ROW * y + (x + d) % ROW) for y in range(ROWS) for x in range(ROW)] for d in range(1, ROW)
}
SWAP = [1, 0, 3, 2]
TURN = [3, 2, 1, 0]
Y_SWAP = [(ROW * y + x, ROW * SWAP[y] + x) for y in range(ROWS) for x in range(ROW)]
Y_TURN = [(ROW * y + x, ROW * TURN[y] + x) for y in range(ROWS) for x in range(ROW)]
ROW_BANDS = [[(ROW * y + x) * BANDS + z for x in range(ROW) for z in range(BANDS)] for y in range(ROWS)]


def shift_x(value, by):
    return lax.ppermute(value, "sweep", X_RING[by % ROW])


def call(body, outs, *args, scratch=()):
    scalar = pl.BlockSpec(memory_space=pltpu.SMEM)
    vector = pl.BlockSpec(memory_space=pltpu.VMEM)
    return pl.pallas_call(
        body,
        out_shape=[jax.ShapeDtypeStruct(shape, dtype) for shape, dtype in outs],
        in_specs=[scalar if arg.ndim == 1 else vector for arg in args],
        out_specs=[vector] * len(outs),
        scratch_shapes=list(scratch),
        compiler_params=PARAMS,
    )(*args)


def place():
    at = lax.axis_index("sweep")
    return at % ROW, at // ROW


def split(value):
    high = value.astype(BF16)
    return high, (value - high.astype(F32)).astype(BF16)


def times(rows, high, low, dims):
    rows_high, rows_low = split(rows)
    count = rows.shape[0]
    both = lax.dot_general(
        jnp.concatenate([rows_high, rows_low], axis=0), high, dims, preferred_element_type=F32
    )
    cross = lax.dot_general(rows_high, low, dims, preferred_element_type=F32)
    return both[:count] + (both[count:] + cross)


def spread_body(coeff, table, source, response, before, after, sky, classes, blocked, f0, f1, f2, f3, s0, s1, s2, s3, sky_rays):
    x, y = place()
    upsun = y < 2
    density = jnp.zeros((1, K), F32)
    for at in range(table.shape[0]):
        density = jnp.where(classes[...] == at, table[at], density)
    transmit = (1 - blocked[...]).astype(F32) * jnp.exp(-coeff[0] * density)
    scale = 1.0 / math.sqrt(R)
    for dist, (first, second) in enumerate(((f0, s0), (f1, s1), (f2, s2), (f3, s3))):
        cols = pl.ds(pl.multiple_of((x + dist) % ROW * CH, CH), CH)
        weights = response[:, cols]
        up = jnp.concatenate([before[:, cols], weights[:-FV]], axis=0)
        down = jnp.concatenate([weights[FV:], after[:, cols]], axis=0)
        cotangent = ((0.5 * weights + 0.25 * (up + down)) * scale).T
        emitted = source[:, cols].T
        first[:CH] = jnp.where(upsun, emitted, cotangent)
        first[CH:] = jnp.broadcast_to(transmit, (SPARE, K))
        second[...] = jnp.where(upsun, cotangent, emitted)
    sky_rays[...] = sky[:, pl.ds(pl.multiple_of(x * CH, CH), CH)].T


def held_at(high, low):
    return lambda rows, j, dims: times(rows, high[j], low[j], dims)


def forward_chain(apply, thin, emitted, incoming, keep, first=0):
    def step(j, state):
        gained = apply(state, j, NT) * thin[j]
        state = gained + emitted[j]
        keep(j, gained, state)
        return state

    return lax.fori_loop(first, ROW, step, incoming, unroll=True)


def backward_chain(apply, thin, cotangent, incoming, keep, through):
    def step(i, state):
        j = ROW - 1 - i
        adjoint = cotangent[j] + state
        keep(j, adjoint)
        return apply(adjoint * thin[j], j, NN)

    state = lax.fori_loop(0, ROW - 1, step, incoming, unroll=True)
    adjoint = cotangent[0] + state
    keep(0, adjoint)
    if through:
        return apply(adjoint * thin[0], 0, NN)
    return None


def cut_body(left, right, e1, e2, e3, far_top, far_bottom):
    far_top[...] = left[:K // 2]
    far_bottom[...] = right[K // 2:]


def near_body(own, left, right, e0, e1, e2, e3, sky_rays,
              high, low, thin, given, part_high, part_low, before_far, after_far):
    x, y = place()
    far = (x + 2) % ROW
    for dist, part in enumerate((e0, e1, e2, e3)):
        tile = (x - dist + ROW) % ROW
        given[tile] = part[:CH]
        thin[tile] = part[CH:CH + 1]
    for dist, part in ((0, own), (1, left), (3, right)):
        tile = (x - dist + ROW) % ROW
        high[tile], low[tile] = split(part[...])

    apply = held_at(high, low)
    inner = (y == 1) | (y == 2)
    first = jnp.where(inner, jnp.where(x < 2, 0, 2), jnp.where(y == 0, far + 1, 0))
    last = jnp.where(inner, first + 1, jnp.where(y == 0, ROW - 1, far - 1))

    @pl.when(first <= last)
    def _():
        part_high[...] = high[first]
        part_low[...] = low[first]

        @pl.loop(first + 1, last + 1)
        def _(j):
            rows = (high[j].astype(F32) + low[j].astype(F32)) * thin[j - 1]
            part_high[...], part_low[...] = split(times(rows, part_high[...], part_low[...], NN))

    def forward(j, state):
        return apply(state, j, NT) * thin[j] + given[j]

    @pl.when(y == 0)
    def _():
        before_far[...] = lax.fori_loop(0, far, forward, sky_rays[...])

        @pl.when(far < ROW - 1)
        def _():
            after_far[...] = lax.fori_loop(far + 2, ROW, forward, given[far + 1])

    def backward_from(top):
        def backward(i, state):
            j = top - i
            return apply((given[j] + state) * thin[j], j, NN)

        return backward

    @pl.when(y == ROWS - 1)
    def _():
        nothing = jnp.zeros((CH, K), F32)
        before_far[...] = lax.fori_loop(0, ROW - 1 - far, backward_from(ROW - 1), nothing)
        after_far[...] = lax.fori_loop(0, far, backward_from(far - 1), nothing)


def start_body(far_top, far_bottom, thin, given, part_high, part_low, before_far, after_far, far_high, far_low, out):
    x, y = place()
    far = (x + 2) % ROW
    far_high[:K // 2], far_low[:K // 2] = split(far_top[...])
    far_high[K // 2:], far_low[K // 2:] = split(far_bottom[...])

    @pl.when(y == 0)
    def _():
        state = times(before_far[...], far_high[...], far_low[...], NT) * thin[far] + given[far]
        out[...] = state

        @pl.when(far < ROW - 1)
        def _():
            out[...] = times(state, part_high[...], part_low[...], NT) * thin[ROW - 1] + after_far[...]

    @pl.when(y == ROWS - 1)
    def _():
        state = times((given[far] + before_far[...]) * thin[far], far_high[...], far_low[...], NN)
        out[...] = state

        @pl.when(far > 0)
        def _():
            out[...] = times(state * thin[far - 1], part_high[...], part_low[...], NN) + after_far[...]


def ends(high, low, thin, given, y, forward_row, out):
    @pl.when(y == forward_row)
    def _():
        out[...] = forward_chain(held_at(high, low), thin, given, given[0], lambda j, g, s: None, 1)

    @pl.when(y == ROWS - 1 - forward_row)
    def _():
        out[...] = backward_chain(held_at(high, low), thin, given, jnp.zeros((CH, K), F32), lambda j, a: None, True)


def ends_body(near_high, near_low, far_high, far_low, thin, given, pair_high, pair_low, sky_rays,
              high, low, whole_high, whole_low, added, saved, radiance):
    x, y = place()
    far = (x + 2) % ROW
    for j in range(ROW):
        @pl.when(j == far)
        def _():
            high[j] = far_high[...]
            low[j] = far_low[...]

        @pl.when(j != far)
        def _():
            high[j] = near_high[j]
            low[j] = near_low[j]

    @pl.when(y == 0)
    def _():
        def keep(j, gained, state):
            saved[j] = gained
            radiance[j] = state

        forward_chain(held_at(high, low), thin, given, sky_rays[...], keep)

    @pl.when(y == ROWS - 1)
    def _():
        def keep(j, adjoint):
            saved[j] = adjoint

        backward_chain(held_at(high, low), thin, given, jnp.zeros((CH, K), F32), keep, False)

    @pl.when((y == 1) | (y == 2))
    def _():
        base = jnp.where(x < 2, 2, 0)
        rows = (high[base + 1].astype(F32) + low[base + 1].astype(F32)) * thin[base]
        far_pair = times(rows, high[base], low[base], NN)

        @pl.when(x < 2)
        def _():
            whole = times(far_pair * thin[1], pair_high[...], pair_low[...], NN)
            whole_high[...], whole_low[...] = split(whole)

        @pl.when(x >= 2)
        def _():
            rows = (pair_high[...].astype(F32) + pair_low[...].astype(F32)) * thin[1]
            first_high, first_low = split(far_pair)
            whole_high[...], whole_low[...] = split(times(rows, first_high, first_low, NN))

    ends(high, low, thin, given, y, 1, added)


def later_body(high, low, thin, s0, s1, s2, s3, given, added):
    x, y = place()
    for dist, part in enumerate((s0, s1, s2, s3)):
        given[(x - dist + ROW) % ROW] = part[...]
    ends(high, low, thin, given, y, 2, added)


def pass_body(forward_row, incoming, whole_high, whole_low, thin, added, out):
    _, y = place()

    @pl.when(y == forward_row)
    def _():
        out[...] = times(incoming[...], whole_high[...], whole_low[...], NT) * thin[ROW - 1] + added[...]

    @pl.when(y == ROWS - 1 - forward_row)
    def _():
        out[...] = times(incoming[...] * thin[ROW - 1], whole_high[...], whole_low[...], NN) + added[...]


def middle_body(high, low, thin, given, later, first_in, second_in, radiance, along, saved):
    _, y = place()
    for row, emitted, cotangent, state, adjoint_in in (
        (1, given, later, first_in, second_in),
        (2, later, given, second_in, first_in),
    ):
        @pl.when(y == row)
        def _():
            def keep_state(j, gained, new_state):
                saved[j] = gained
                radiance[j] = new_state

            def keep_adjoint(j, adjoint):
                along[j] = jnp.sum(adjoint * saved[j], axis=0, keepdims=True)

            forward_chain(held_at(high, low), thin, emitted, state[...], keep_state)
            backward_chain(held_at(high, low), thin, cotangent, adjoint_in[...], keep_adjoint, False)


def last_body(high, low, thin, later, last_in, early, middle, gain, x0, x1, x2, x3, held):
    x, y = place()
    outs = (x0, x1, x2, x3)

    @pl.when(y == ROWS - 1)
    def _():
        def keep(j, gained, state):
            gain[j] = gained
            held[j] = state

        forward_chain(held_at(high, low), thin, later, last_in[...], keep)
        for dist, out in enumerate(outs):
            out[...] = held[(x + dist) % ROW]

    @pl.when(y == 0)
    def _():
        for dist, out in enumerate(outs):
            out[...] = early[(x + dist) % ROW]

    @pl.when((y == 1) | (y == 2))
    def _():
        for dist, out in enumerate(outs):
            out[...] = middle[(x + dist) % ROW]


def along_body(coeff, high, low, thin, later, last_in, saved, gain, middle_along, out, along):
    x, y = place()
    factor = -coeff[0]

    @pl.when(y == 0)
    def _():
        def keep(j, adjoint):
            along[j] = jnp.sum(adjoint * saved[j], axis=0, keepdims=True)

        backward_chain(held_at(high, low), thin, later, last_in[...], keep, False)

    @pl.when(y == ROWS - 1)
    def _():
        for j in range(ROW):
            along[j] = jnp.sum(gain[j] * saved[j], axis=0, keepdims=True)

    @pl.when((y == 1) | (y == 2))
    def _():
        for j in range(ROW):
            along[j] = middle_along[j]

    for j in range(ROW):
        out[j * BANDS:(j + 1) * BANDS] = jnp.broadcast_to((factor * along[j])[None], (BANDS, 1, K))


def rim_body(r0, r1, r2, r3, edge):
    x, _ = place()
    low_side = lax.axis_index("cross") == 0
    for dist, part in enumerate((r0, r1, r2, r3)):
        cols = pl.ds(pl.multiple_of((x - dist + ROW) % ROW * CH, CH), CH)
        edge[:, cols] = jnp.where(low_side, part[:, K - FV:], part[:, :FV]).T


def turn_body(r0, r1, r2, r3, out):
    x, _ = place()
    for dist, part in enumerate((r0, r1, r2, r3)):
        cols = pl.ds(pl.multiple_of((x - dist + ROW) % ROW * CH, CH), CH)
        out[:, cols] = part[...].T


def smooth_body(grid, edge, out, done):
    low_side = lax.axis_index("cross") == 0
    whole = grid[...]
    halo = edge[...]
    up = jnp.concatenate([jnp.where(low_side, 0.0, halo), whole[:-FV]], axis=0)
    down = jnp.concatenate([whole[FV:], jnp.where(low_side, halo, 0.0)], axis=0)
    out[...] = 0.5 * whole + 0.25 * (up + down)
    done[...] = halo[:8, :128]


def total_body(lines, done, out):
    out[...] = jnp.sum(lines[...], axis=0)


def per_device(operator, source, sky, response, extinction, leaf_density, leaf_class, occupied):
    local = operator[0, 0]
    weights = response[0, 0]
    side = lax.axis_index("cross")
    other_side = [(0, 1), (1, 0)]

    left = shift_x(local, 1)
    right = shift_x(local, -1)

    edge = lax.ppermute(jnp.where(side == 0, weights[-FV:], weights[:FV]), "cross", other_side)
    before = jnp.where(side == 1, edge, 0.0)
    after = jnp.where(side == 0, edge, 0.0)
    part = ((CH, K), F32)
    chunk = ((ROW, CH, K), F32)
    line = ((ROW, 1, K), F32)
    first = ((CH + SPARE, K), F32)
    f0, f1, f2, f3, s0, s1, s2, s3, sky_rays = call(
        spread_body, [first] * ROW + [part] * (ROW + 1),
        extinction, leaf_density, source[0, 0], weights, before, after, sky[0], leaf_class, occupied)
    e0 = f0
    e2 = shift_x(f2, 2)
    e3 = shift_x(f3, 3)
    e1 = shift_x(f1, 1)
    half = ((K // 2, K), F32)
    operators = ((ROW, K, K), BF16)
    whole = ((K, K), BF16)
    far_top, far_bottom = call(cut_body, [half, half], left, right, e1, e2, e3)
    far_bottom = shift_x(far_bottom, -1)
    far_top = shift_x(far_top, 1)
    near_high, near_low, thin, given, part_high, part_low, before_far, after_far = call(
        near_body, [operators, operators, line, chunk, whole, whole, part, part],
        local, left, right, e0, e1, e2, e3, sky_rays)
    far_high, far_low, out = call(
        start_body, [whole, whole, part],
        far_top, far_bottom, thin, given, part_high, part_low, before_far, after_far)
    first_in = lax.ppermute(out, "sweep", Y_SWAP)
    s1, s2, s3 = shift_x(s1, 1), shift_x(s2, 2), shift_x(s3, 3)
    high, low, whole_high, whole_low, added, saved, early = call(
        ends_body, [operators, operators, whole, whole, part, chunk, chunk],
        near_high, near_low, far_high, far_low, thin, given, part_high, part_low, sky_rays)
    (out,) = call(functools.partial(pass_body, 1), [part], first_in, whole_high, whole_low, thin, added)
    second_in = lax.ppermute(out, "sweep", Y_TURN)
    later, added = call(later_body, [chunk, part], high, low, thin, s0, s1, s2, s3)
    (out,) = call(functools.partial(pass_body, 2), [part], second_in, whole_high, whole_low, thin, added)
    last_in = lax.ppermute(out, "sweep", Y_SWAP)
    held = pltpu.VMEM((ROW, CH, K), F32)
    middle, middle_along = call(
        middle_body, [chunk, line], high, low, thin, given, later, first_in, second_in, scratch=[held])
    gain, x0, x1, x2, x3 = call(
        last_body, [chunk] + [part] * ROW, high, low, thin, later, last_in, early, middle, scratch=[held])
    r0, r1, r2, r3 = x0, shift_x(x1, 1), shift_x(x2, 2), shift_x(x3, 3)
    (lines,) = call(
        along_body, [((ROW * BANDS, 1, K), F32)], extinction, high, low, thin, later, last_in, saved, gain, middle_along,
        scratch=[pltpu.VMEM((ROW, 1, K), F32)])
    lines = lax.all_to_all(lines, ("sweep", "band"), 0, 0, axis_index_groups=ROW_BANDS)

    (edge,) = call(rim_body, [((FV, R), F32)], r0, r1, r2, r3)
    edge = lax.ppermute(edge, "cross", other_side)
    (grid,) = call(turn_body, [((K, R), F32)], r0, r1, r2, r3)
    observed, done = call(smooth_body, [((K, R), F32), ((8, 128), F32)], grid, edge)
    (total,) = call(total_body, [((1, K), F32)], lines, done)
    return (observed[None, None], total)


def solution(mesh):
    in_specs = (
        P("band", "sweep", "cross", None),
        P("band", "sweep", "cross", None),
        P("band", "cross", None),
        P("band", "sweep", "cross", None),
        P("band"),
        P(),
        P("sweep", "cross"),
        P("sweep", "cross"),
    )
    out_specs = (P("band", "sweep", "cross", None), P("sweep", "cross"))
    return jax.shard_map(
        per_device, mesh=mesh, in_specs=in_specs, out_specs=out_specs, check_vma=False
    )
```
